32 devices in a mesh: work: 8 (over z, y), rep: 4 (over x, core).
Axes of the slice: x: 2, y: 2, z: 4, core: 2. Of those that a mesh axis runs over, the one named last changes fastest.
Arguments:
- gradients: bfloat16 [256, 512, 512], P('work', None, 'rep'), may hold values from -6 to 6
- output_stats: bfloat16 [8, 128, 512], P('work', 'rep'), may hold values from -6 to 6
- input_stats: bfloat16 [8, 128, 512], P('work', 'rep'), may hold values from -6 to 6
- output_factor: float32 [8, 512, 512], P('work')
- output_inverse: float32 [8, 512, 512], P('work')
- input_factor: float32 [8, 512, 512], P('work')
- input_inverse: float32 [8, 512, 512], P('work')
- block_output: int32 [256], replicated, may hold values from 0 to 7, as said below
- block_input: int32 [256], replicated, may hold values from 0 to 7, as said below
- output_owner: int32 [8], replicated, may hold values from 0 to 7, each once
- input_owner: int32 [8], replicated, may hold values from 0 to 7, each once
Outputs:
- preconditioned: bfloat16 [256, 512, 512], P('work', 'rep')
The draws below stay inside these ranges and needn't reach their ends.
Inputs may be any that keep to these rules, and one draw needn't show every extreme that they name: `block_output`: among the 32 blocks of one home, no output factor is named more than 4 times, and some factor is named exactly 4 times; the same holds for input factors. No pair of an output factor and an input factor is named by more than 4 blocks in all. Every output factor and every input factor is named by exactly 32 blocks in all. `block_input`: drawn together with block_output; see there.
All inputs are finite; a program needn't handle non-finite values.
Results may differ from the reference program's by a relative error of at most 0.0067.
Values may be sent and summed in bfloat16 or wider, within the bound.
A program may use at most 128 MiB of HBM per device.

```python
import math
import jax
import jax.numpy as jnp
from jax import lax

B = 512
BLK_DEV = 32
NFACT = 8
NBLK = 256
ROWS = 128


def dominant(key, diag_low, diag_high, spread, symmetric):
    first_key, second_key = jax.random.split(key)
    diagonal = jax.random.uniform(first_key, (NFACT, B), jnp.float32, diag_low, diag_high)
    jitter = jax.random.normal(second_key, (NFACT, B, B), jnp.float32) * (spread / math.sqrt(B))
    if symmetric:
        jitter = (jitter + jnp.swapaxes(jitter, 1, 2)) / math.sqrt(2.0)
    return jitter + diagonal[:, :, None] * jnp.eye(B, dtype=jnp.float32)[None, :, :]


def draw_output_factor(key, part):
    inner_key = jax.random.fold_in(key, 101)
    return dominant(inner_key, 1.5, 3.0, 0.5, True)


def draw_input_factor(key, part):
    inner_key = jax.random.fold_in(key, 202)
    return dominant(inner_key, 1.5, 3.0, 0.5, True)


def draw_output_inverse(key, part):
    inner_key = jax.random.fold_in(key, 303)
    return dominant(inner_key, 0.35, 0.6, 0.15, False)


def draw_input_inverse(key, part):
    inner_key = jax.random.fold_in(key, 404)
    return dominant(inner_key, 0.35, 0.6, 0.15, False)


def block_pairs(key):
    base_key = jax.random.fold_in(key, 11)
    key_list = jax.random.split(base_key, 5)
    home_count = NBLK // BLK_DEV
    levels = NFACT.bit_length() - 1
    scores = jax.random.randint(key_list[0], (home_count, BLK_DEV), 0, 1 << 20) * BLK_DEV + jnp.arange(BLK_DEV, dtype=jnp.int32)[None, :]
    shuffled = jnp.argsort(scores, axis=1).astype(jnp.int32)
    chosen = jax.random.permutation(key_list[1], NFACT).astype(jnp.int32)
    picked = chosen[shuffled % NFACT]
    feedback = (picked >> levels - 1 & 1) * 3
    twisted = picked << 1 & NFACT - 1 ^ feedback
    home_shift = jax.random.permutation(key_list[2], NFACT).astype(jnp.int32)[:, None]
    out_point = (home_shift ^ picked).reshape(NBLK)
    in_point = (home_shift ^ picked ^ twisted).reshape(NBLK)
    out_labels = jax.random.permutation(key_list[3], NFACT).astype(jnp.int32)
    in_labels = jax.random.permutation(key_list[4], NFACT).astype(jnp.int32)
    return (out_labels[out_point], in_labels[in_point])


def draw_block_output(key, part):
    return block_pairs(key)[0]


def draw_block_input(key, part):
    return block_pairs(key)[1]


def block_levels(rng, extent, shards, low, top_value):
    level = 1.0
    for axis_at, parts in shards:
        heights = jax.random.uniform(jax.random.fold_in(jax.random.fold_in(rng, 6), axis_at), (parts,), jnp.float32, low / len(shards), top_value / len(shards))
        level = level * jnp.repeat(jnp.exp(heights), extent[axis_at] // parts).reshape((-1,) + (1,) * (len(extent) - 1 - axis_at))
    return level


def bell_draw(stream_key, shape, deviation, limit, cuts=(), kind=jnp.bfloat16):
    result = jax.random.normal(stream_key, shape, jnp.float32) * deviation
    if len(cuts) > 0:
        result = block_levels(stream_key, shape, cuts, -0.22, 0.18) * result
    return jnp.clip(result, min=-limit, max=limit).astype(kind)


def setup_inputs(seed: int = 0) -> dict:
    streams_of = jax.random.split(jax.random.key(seed), 12)
    gradients = bell_draw(streams_of[0], (NBLK, B, B), 1.0, 6.0, ((0, 8), (2, 4)))
    output_stats = bell_draw(streams_of[1], (NFACT, ROWS, B), 1.0, 6.0, ((0, 8), (1, 4)))
    input_stats = bell_draw(streams_of[2], (NFACT, ROWS, B), 1.0, 6.0, ((0, 8), (1, 4)))
    output_factor = draw_output_factor(jax.random.fold_in(streams_of[11], 71), 0)
    output_inverse = draw_output_inverse(jax.random.fold_in(streams_of[11], 71), 0)
    input_factor = draw_input_factor(jax.random.fold_in(streams_of[11], 71), 0)
    input_inverse = draw_input_inverse(jax.random.fold_in(streams_of[11], 71), 0)
    block_output = draw_block_output(jax.random.fold_in(streams_of[11], 71), 0)
    block_input = draw_block_input(jax.random.fold_in(streams_of[11], 71), 0)
    output_owner = jax.random.permutation(streams_of[9], NFACT).astype(jnp.int32)
    input_owner = jax.random.permutation(streams_of[10], NFACT).astype(jnp.int32)
    return {"gradients": gradients, "output_stats": output_stats, "input_stats": input_stats, "output_factor": output_factor, "output_inverse": output_inverse, "input_factor": input_factor, "input_inverse": input_inverse, "block_output": block_output, "block_input": block_input, "output_owner": output_owner, "input_owner": input_owner}


decay_rate = 0.5


def refine(factor, inverse, samples):
    moment = jnp.dot(samples.T, samples, preferred_element_type=jnp.float32)
    updated = decay_rate * factor + ((1.0 - decay_rate) / samples.shape[0]) * moment
    product = jnp.dot(updated, inverse, precision=lax.Precision.HIGHEST)
    refined = 2.0 * inverse - jnp.dot(inverse, product, precision=lax.Precision.HIGHEST)
    return refined.astype(jnp.bfloat16)


def reference(gradients, output_stats, input_stats, output_factor, output_inverse, input_factor, input_inverse, block_output, block_input, output_owner, input_owner):
    left_all = lax.map(lambda entries: refine(entries[0], entries[1], entries[2]), (output_factor, output_inverse, output_stats))
    right_all = lax.map(lambda entries: refine(entries[0], entries[1], entries[2]), (input_factor, input_inverse, input_stats))
    left_place = output_owner[block_output].astype(jnp.int32)
    right_place = input_owner[block_input].astype(jnp.int32)

    def precondition(entries):
        single_block, left_index, right_index = entries
        middle = jnp.dot(left_all[left_index], single_block, preferred_element_type=jnp.float32).astype(jnp.bfloat16)
        return jnp.dot(middle, right_all[right_index], preferred_element_type=jnp.float32).astype(jnp.bfloat16)

    return lax.map(precondition, (gradients, left_place, right_place))
```

```python
import jax
import jax.numpy as jnp
from jax import lax
from jax.sharding import PartitionSpec as P

decay_rate = 0.5


def refine(factor, inverse, samples):
    moment = jnp.dot(samples.T, samples, preferred_element_type=jnp.float32)
    updated = decay_rate * factor + (1.0 - decay_rate) / samples.shape[0] * moment
    product = jnp.dot(updated, inverse, precision=lax.Precision.HIGHEST)
    refined = 2.0 * inverse - jnp.dot(inverse, product, precision=lax.Precision.HIGHEST)
    return refined.astype(jnp.bfloat16)


def lookup(labels, values):
    matches = labels[:, None] == jnp.arange(values.shape[0], dtype=jnp.int32)[None, :]
    return jnp.sum(jnp.where(matches, values[None, :], 0), axis=1)


def group_rank(grouping):
    count = grouping.shape[0]
    positions = jnp.arange(count, dtype=jnp.int32)
    same_group = grouping[:, None] == grouping[None, :]
    earlier = positions[None, :] < positions[:, None]
    return jnp.sum(jnp.logical_and(same_group, earlier), axis=1)


def place_rows(target, data, out_count):
    selector = (jnp.arange(out_count, dtype=jnp.int32)[:, None] == target[None, :]).astype(
        jnp.bfloat16
    )
    return jnp.einsum("st,tij->sij", selector, data, preferred_element_type=jnp.float32).astype(
        jnp.bfloat16
    )


def pick_rows(source, data):
    selector = (source[:, None] == jnp.arange(data.shape[0], dtype=jnp.int32)[None, :]).astype(
        jnp.bfloat16
    )
    return jnp.einsum("st,tij->sij", selector, data, preferred_element_type=jnp.float32).astype(
        jnp.bfloat16
    )


def redirect(slot_count, holding, source_slot, target_slot):
    chosen = jnp.where(holding, source_slot, slot_count)
    return jnp.full((slot_count,), slot_count, jnp.int32).at[chosen].set(target_slot, mode="drop")


def relocate(buffer, target, slot_count):
    flat_view = buffer.reshape((slot_count,) + buffer.shape[2:])
    placed = place_rows(target, flat_view, slot_count)
    return placed.reshape(buffer.shape)


def exchange_blocks(
    gradients,
    output_stats,
    input_stats,
    output_factor,
    output_inverse,
    input_factor,
    input_inverse,
    block_output,
    block_input,
    output_owner,
    input_owner,
):
    workers = lax.axis_size("work")
    local_blocks, block_order, shard_cols = gradients.shape
    total_blocks = block_output.shape[0]
    capacity = (local_blocks + workers - 1) // workers
    slot_count = workers * capacity
    worker_index = lax.axis_index("work")
    home_index = jnp.arange(total_blocks, dtype=jnp.int32) // local_blocks
    out_dest = lookup(block_output, output_owner)
    in_dest = lookup(block_input, input_owner)
    first_rank = group_rank(home_index * workers + out_dest)
    second_rank = group_rank(out_dest * workers + in_dest)
    third_rank = group_rank(in_dest * workers + home_index)
    gathered_out, gathered_in = (
        lax.all_gather(output_stats, "rep", axis=1, tiled=True),
        lax.all_gather(input_stats, "rep", axis=1, tiled=True),
    )
    left_inverse = refine(output_factor[0], output_inverse[0], gathered_out[0])
    right_inverse = refine(input_factor[0], input_inverse[0], gathered_in[0])
    own_places = lax.dynamic_slice_in_dim(
        out_dest * capacity + first_rank, worker_index * local_blocks, local_blocks
    )
    outgoing = place_rows(own_places, gradients, slot_count)
    outgoing = outgoing.reshape(workers, capacity, block_order, shard_cols)
    arrived = jnp.einsum(
        "ij,nkjc->nkic",
        left_inverse,
        lax.all_to_all(outgoing, "work", split_axis=0, concat_axis=0, tiled=True),
        preferred_element_type=jnp.float32,
    ).astype(jnp.bfloat16)
    second_target = redirect(
        slot_count,
        out_dest == worker_index,
        home_index * capacity + first_rank,
        in_dest * capacity + second_rank,
    )
    forward = relocate(arrived, second_target, slot_count)
    third_target = redirect(
        slot_count,
        in_dest == worker_index,
        out_dest * capacity + second_rank,
        home_index * capacity + third_rank,
    )
    rows_form = lax.all_to_all(forward, "rep", split_axis=2, concat_axis=3, tiled=True)
    finished = jnp.einsum(
        "nkrc,cd->nkrd",
        lax.all_to_all(rows_form, "work", split_axis=0, concat_axis=0, tiled=True),
        right_inverse,
        preferred_element_type=jnp.float32,
    ).astype(jnp.bfloat16)
    backward = relocate(finished, third_target, slot_count)
    returned = lax.all_to_all(backward, "work", split_axis=0, concat_axis=0, tiled=True)
    returned = returned.reshape((slot_count,) + returned.shape[2:])
    own_slots = lax.dynamic_slice_in_dim(
        in_dest * capacity + third_rank, worker_index * local_blocks, local_blocks
    )
    return pick_rows(own_slots, returned)


def gather_factors(
    gradients,
    output_stats,
    input_stats,
    output_factor,
    output_inverse,
    input_factor,
    input_inverse,
    block_output,
    block_input,
    output_owner,
    input_owner,
):
    workers = lax.axis_size("work")
    replicas = lax.axis_size("rep")
    local_blocks, block_order, shard_cols = gradients.shape
    capacity = (local_blocks + workers - 1) // workers
    slot_count = workers * capacity
    work, rep = lax.axis_index("work"), lax.axis_index("rep")
    start = work * local_blocks
    out_dest = lookup(lax.dynamic_slice_in_dim(block_output, start, local_blocks), output_owner)
    in_dest = lookup(lax.dynamic_slice_in_dim(block_input, start, local_blocks), input_owner)
    out_slot = out_dest * capacity + group_rank(out_dest)
    in_slot = in_dest * capacity + group_rank(in_dest)
    blocks = jnp.arange(local_blocks, dtype=jnp.int32)
    out_block = jnp.zeros((slot_count,), jnp.int32).at[out_slot].set(blocks)
    in_block = jnp.zeros((slot_count,), jnp.int32).at[in_slot].set(blocks)
    share = block_order // replicas
    samples = lax.all_gather(
        jnp.concatenate([output_stats, input_stats], 0), "rep", axis=1, tiled=True
    )

    def part(factor, inverse, rows):
        moment = jnp.dot(rows.T, rows, preferred_element_type=jnp.float32)
        updated = decay_rate * factor + (1.0 - decay_rate) / rows.shape[0] * moment
        own = lax.dynamic_slice_in_dim(inverse, rep * share, share)
        product = jnp.dot(own, updated, precision=lax.Precision.HIGHEST)
        refined = 2.0 * own - jnp.dot(product, inverse, precision=lax.Precision.HIGHEST)
        return refined.astype(jnp.bfloat16)

    left = part(output_factor[0], output_inverse[0], samples[0])
    right = part(input_factor[0], input_inverse[0], samples[1])
    shape = (workers, block_order, block_order)
    left = lax.all_gather(left, ("work", "rep"), axis=0, tiled=True).reshape(shape)
    right = lax.all_gather(right, ("work", "rep"), axis=0, tiled=True).reshape(shape)
    sorted_blocks = pick_rows(out_block, gradients).reshape(workers, capacity, block_order, shard_cols)
    middle = jnp.einsum(
        "wij,wkjc->wkic", left, sorted_blocks, preferred_element_type=jnp.float32
    ).astype(jnp.bfloat16)
    middle = middle.reshape(slot_count, block_order, shard_cols)
    rows_form = lax.all_to_all(middle, "rep", split_axis=1, concat_axis=2, tiled=True)
    rows_form = pick_rows(lookup(in_block, out_slot), rows_form).reshape(workers, capacity * share, block_order)
    finished = jnp.einsum(
        "wrc,wcd->wrd", rows_form, right, preferred_element_type=jnp.float32
    ).astype(jnp.bfloat16)
    return pick_rows(in_slot, finished.reshape(slot_count, share, block_order))


def solution(mesh):
    in_specs = (
        P("work", None, "rep"),
        P("work", "rep", None),
        P("work", "rep", None),
        P("work", None, None),
        P("work", None, None),
        P("work", None, None),
        P("work", None, None),
        P(),
        P(),
        P(),
        P(),
    )
    out_specs = P("work", "rep", None)
    local = gather_factors if mesh.shape["work"] <= 16 else exchange_blocks
    return jax.shard_map(local, mesh=mesh, in_specs=in_specs, out_specs=out_specs, check_vma=False)
```

```python
import functools

import jax
import jax.numpy as jnp
from jax import lax
from jax.experimental import pallas as pl
from jax.experimental.pallas import tpu as pltpu
from jax.sharding import PartitionSpec as P

decay_rate = 0.5


def refine(factor, inverse, samples):
    moment = jnp.dot(samples.T, samples, preferred_element_type=jnp.float32)
    updated = decay_rate * factor + (1.0 - decay_rate) / samples.shape[0] * moment
    product = jnp.dot(updated, inverse, precision=lax.Precision.HIGHEST)
    refined = 2.0 * inverse - jnp.dot(inverse, product, precision=lax.Precision.HIGHEST)
    return refined.astype(jnp.bfloat16)


def lookup(labels, values):
    matches = labels[:, None] == jnp.arange(values.shape[0], dtype=jnp.int32)[None, :]
    return jnp.sum(jnp.where(matches, values[None, :], 0), axis=1)


def group_rank(grouping):
    count = grouping.shape[0]
    positions = jnp.arange(count, dtype=jnp.int32)
    same_group = grouping[:, None] == grouping[None, :]
    earlier = positions[None, :] < positions[:, None]
    return jnp.sum(jnp.logical_and(same_group, earlier), axis=1)


def place_rows(target, data, out_count):
    selector = (jnp.arange(out_count, dtype=jnp.int32)[:, None] == target[None, :]).astype(
        jnp.bfloat16
    )
    return jnp.einsum("st,tij->sij", selector, data, preferred_element_type=jnp.float32).astype(
        jnp.bfloat16
    )


def pick_rows(source, data):
    selector = (source[:, None] == jnp.arange(data.shape[0], dtype=jnp.int32)[None, :]).astype(
        jnp.bfloat16
    )
    return jnp.einsum("st,tij->sij", selector, data, preferred_element_type=jnp.float32).astype(
        jnp.bfloat16
    )


def redirect(slot_count, holding, source_slot, target_slot):
    chosen = jnp.where(holding, source_slot, slot_count)
    return jnp.full((slot_count,), slot_count, jnp.int32).at[chosen].set(target_slot, mode="drop")


def relocate(buffer, target, slot_count):
    flat_view = buffer.reshape((slot_count,) + buffer.shape[2:])
    placed = place_rows(target, flat_view, slot_count)
    return placed.reshape(buffer.shape)


def exchange_blocks(
    gradients,
    output_stats,
    input_stats,
    output_factor,
    output_inverse,
    input_factor,
    input_inverse,
    block_output,
    block_input,
    output_owner,
    input_owner,
):
    workers = lax.axis_size("work")
    local_blocks, block_order, shard_cols = gradients.shape
    total_blocks = block_output.shape[0]
    capacity = (local_blocks + workers - 1) // workers
    slot_count = workers * capacity
    worker_index = lax.axis_index("work")
    home_index = jnp.arange(total_blocks, dtype=jnp.int32) // local_blocks
    out_dest = lookup(block_output, output_owner)
    in_dest = lookup(block_input, input_owner)
    first_rank = group_rank(home_index * workers + out_dest)
    second_rank = group_rank(out_dest * workers + in_dest)
    third_rank = group_rank(in_dest * workers + home_index)
    gathered_out, gathered_in = (
        lax.all_gather(output_stats, "rep", axis=1, tiled=True),
        lax.all_gather(input_stats, "rep", axis=1, tiled=True),
    )
    left_inverse = refine(output_factor[0], output_inverse[0], gathered_out[0])
    right_inverse = refine(input_factor[0], input_inverse[0], gathered_in[0])
    own_places = lax.dynamic_slice_in_dim(
        out_dest * capacity + first_rank, worker_index * local_blocks, local_blocks
    )
    outgoing = place_rows(own_places, gradients, slot_count)
    outgoing = outgoing.reshape(workers, capacity, block_order, shard_cols)
    arrived = jnp.einsum(
        "ij,nkjc->nkic",
        left_inverse,
        lax.all_to_all(outgoing, "work", split_axis=0, concat_axis=0, tiled=True),
        preferred_element_type=jnp.float32,
    ).astype(jnp.bfloat16)
    second_target = redirect(
        slot_count,
        out_dest == worker_index,
        home_index * capacity + first_rank,
        in_dest * capacity + second_rank,
    )
    forward = relocate(arrived, second_target, slot_count)
    third_target = redirect(
        slot_count,
        in_dest == worker_index,
        out_dest * capacity + second_rank,
        home_index * capacity + third_rank,
    )
    rows_form = lax.all_to_all(forward, "rep", split_axis=2, concat_axis=3, tiled=True)
    finished = jnp.einsum(
        "nkrc,cd->nkrd",
        lax.all_to_all(rows_form, "work", split_axis=0, concat_axis=0, tiled=True),
        right_inverse,
        preferred_element_type=jnp.float32,
    ).astype(jnp.bfloat16)
    backward = relocate(finished, third_target, slot_count)
    returned = lax.all_to_all(backward, "work", split_axis=0, concat_axis=0, tiled=True)
    returned = returned.reshape((slot_count,) + returned.shape[2:])
    own_slots = lax.dynamic_slice_in_dim(
        in_dest * capacity + third_rank, worker_index * local_blocks, local_blocks
    )
    return pick_rows(own_slots, returned)


def flip(value, mask):
    result, bit = value, 1
    while bit <= mask:
        if mask & bit:
            result = result + bit - 2 * bit * ((value // bit) % 2)
        bit *= 2
    return result


def halves(x):
    high = x.astype(jnp.bfloat16)
    return high, (x - high.astype(jnp.float32)).astype(jnp.bfloat16)


def dot(a, b):
    return jnp.dot(a, b, preferred_element_type=jnp.float32)


def exact_dot(a, b):
    return dot(a[0], b[0]) + (dot(a[0], b[1]) + dot(a[1], b[0]))


def fused_kernel(
    workers,
    replicas,
    first_ref,
    second_ref,
    g_ref,
    os_ref,
    is_ref,
    of_ref,
    oi_ref,
    if_ref,
    ii_ref,
    out_ref,
    stats,
    factors,
    middle,
    rows,
    result,
    stat_send,
    stat_recv,
    z_send,
    z_recv,
    y_send,
    y_recv,
    s_send,
    s_recv,
    m_send,
    m_recv,
    out_sem,
):
    work, rep = lax.axis_index("work"), lax.axis_index("rep")
    blocks, order, cols = g_ref.shape
    capacity = blocks // workers
    lines = workers // 2
    share = order // replicas
    half = order // 2
    core = rep % 2
    sibling = {"rep": flip(rep, 1)}
    pending = []

    barrier = pltpu.get_barrier_semaphore()
    peers = [{"rep": flip(rep, d)} for d in range(1, replicas)]
    peers += [{"work": flip(work, 1)}] + [{"work": flip(work, 2 * d)} for d in range(1, lines)]
    for peer in peers:
        pl.semaphore_signal(barrier, inc=1, device_id=peer, device_id_type=pl.DeviceIdType.MESH)
    pl.semaphore_wait(barrier, len(peers))

    def push(src, dst, send, recv, peer):
        copy = pltpu.make_async_remote_copy(
            src_ref=src,
            dst_ref=dst,
            send_sem=send,
            recv_sem=recv,
            device_id=peer,
            device_id_type=pl.DeviceIdType.MESH,
        )
        copy.start()
        pending.append(copy)
        return copy

    stat_copies = []
    for t, ref in enumerate((os_ref, is_ref)):
        for d in range(1, replicas):
            stat_copies.append(
                push(
                    ref.at[0],
                    stats.at[t, rep],
                    stat_send.at[t, d - 1],
                    stat_recv.at[t, d - 1],
                    {"rep": flip(rep, d)},
                )
            )
        stats[t, rep] = ref[0]

    mine = pl.ds(pl.multiple_of(core * half, half), half)
    places = [flip(work, i) for i in range(workers)]

    def chunk(t, i):
        return factors.at[t, places[i], mine]

    def refine_half(t, f_ref, i_ref):
        for copy in stat_copies[t * (replicas - 1) : (t + 1) * (replicas - 1)]:
            copy.wait_recv()
        sample = stats[t].reshape(-1, order)
        moment = lax.dot_general(
            sample, sample, (((0,), (0,)), ((), ())), preferred_element_type=jnp.float32
        )
        updated = decay_rate * f_ref[0] + (1.0 - decay_rate) / sample.shape[0] * moment
        own = i_ref[0, mine]
        product = exact_dot(halves(own), halves(updated))
        refined = 2.0 * own - exact_dot(halves(product), halves(i_ref[0]))
        factors[t, places[0], mine] = refined.astype(jnp.bfloat16)

    z_copies, y_copies, s_copies = {}, {}, {}

    def to_sibling(t, i):
        s_copies[t, i] = push(chunk(t, i), chunk(t, i), s_send.at[t, i], s_recv.at[t, i], sibling)

    def to_y(t, d):
        y_copies[t, d] = push(
            chunk(t, 2 * d),
            chunk(t, 2 * d),
            y_send.at[t, d],
            y_recv.at[t, d],
            {"work": places[1]},
        )

    def to_z(t):
        for d in range(1, lines):
            z_copies[t, d] = push(
                chunk(t, 0),
                chunk(t, 0),
                z_send.at[t, d - 1],
                z_recv.at[t, d - 1],
                {"work": places[2 * d]},
            )

    m_copies = []
    own_cols = pl.ds(pl.multiple_of(rep * cols, cols), cols)
    own_rows = pl.ds(pl.multiple_of(rep * share, share), share)

    def left_multiply(i):
        slots = pl.ds(i * capacity, capacity)
        wide = jnp.concatenate(
            [g_ref[first_ref[i * capacity + k]] for k in range(capacity)], axis=1
        )
        for j in range(2):
            part = pl.ds(j * half, half)
            product = dot(factors[0, places[i], part], wide).astype(jnp.bfloat16)
            for k in range(capacity):
                middle[i * capacity + k, part] = product[:, k * cols : (k + 1) * cols]
        for d in range(replicas - 1, 0, -1):
            other = flip(rep, d)
            m_copies.append(
                push(
                    middle.at[slots, pl.ds(pl.multiple_of(other * share, share), share)],
                    rows.at[slots, :, own_cols],
                    m_send.at[i, d - 1],
                    m_recv.at[i, d - 1],
                    {"rep": other},
                )
            )
        rows[slots, :, own_cols] = middle[slots, own_rows]

    def spread(t, ready):
        done = 0
        queue = [0]
        for d in range(1, lines + 1):
            if d < lines:
                z_copies[t, d].wait_recv()
                to_y(t, d)
                to_sibling(t, 2 * d)
                if d == lines - 1 and t == 0:
                    to_y(1, 0)
                    to_z(1)
                    to_sibling(1, 0)
            while queue:
                i = queue.pop(0)
                s_copies[t, i].wait_recv()
                ready(i)
            y_copies[t, d - 1].wait_recv()
            to_sibling(t, 2 * d - 1)
            if d < lines:
                queue.append(2 * d)
            queue.append(2 * d - 1)
        for i in queue:
            s_copies[t, i].wait_recv()
            ready(i)

    refine_half(0, of_ref, oi_ref)
    to_y(0, 0)
    to_z(0)
    to_sibling(0, 0)
    refine_half(1, if_ref, ii_ref)
    spread(0, left_multiply)
    whole = []
    spread(1, whole.append)
    for copy in m_copies:
        copy.wait_recv()
    out_copies = []
    for i in range(workers):
        slots = pl.ds(i * capacity, capacity)
        for k in range(0, capacity, 2):
            pair = [rows[second_ref[i * capacity + k + j]] for j in range(min(2, capacity - k))]
            product = dot(jnp.concatenate(pair, axis=0), factors[1, places[i]])
            for j in range(len(pair)):
                result[i * capacity + k + j] = product[j * share : (j + 1) * share].astype(
                    jnp.bfloat16
                )
        copy = pltpu.make_async_copy(result.at[slots], out_ref.at[slots], out_sem.at[i])
        copy.start()
        out_copies.append(copy)
    for copy in out_copies:
        copy.wait()
    for copy in pending:
        copy.wait_send()


def permute_kernel(place_ref, in_ref, out_ref, sems):
    copies = []
    for b in range(in_ref.shape[0]):
        copy = pltpu.make_async_copy(in_ref.at[place_ref[b]], out_ref.at[b], sems.at[b])
        copy.start()
        copies.append(copy)
    for copy in copies:
        copy.wait()


def gather_factors(
    gradients,
    output_stats,
    input_stats,
    output_factor,
    output_inverse,
    input_factor,
    input_inverse,
    block_output,
    block_input,
    output_owner,
    input_owner,
):
    workers, replicas = lax.axis_size("work"), lax.axis_size("rep")
    blocks, order, cols = gradients.shape
    capacity = blocks // workers
    share = order // replicas
    work = lax.axis_index("work")
    labels = jnp.stack([block_output, block_input]).reshape(2, workers, blocks)
    labels = lax.dynamic_index_in_dim(labels, work, 1, keepdims=False)
    owners = jnp.stack([output_owner, input_owner]) ^ work
    choices = jnp.arange(owners.shape[1], dtype=jnp.int32)
    dest = jnp.sum(jnp.where(labels[:, :, None] == choices, owners[:, None, :], 0), axis=2)
    at = jnp.arange(blocks, dtype=jnp.int32)
    same = (dest[:, :, None] == dest[:, None, :]) & (at[None, :] < at[:, None])
    slot = dest * capacity + jnp.sum(same, axis=2)
    held = slot[:, None, :] == at[:, None]
    first = jnp.sum(jnp.where(held[0], at, 0), axis=1)
    second = jnp.sum(jnp.where(held[1], slot[0], 0), axis=1)
    smem = pl.BlockSpec(memory_space=pltpu.SMEM)
    vmem = pl.BlockSpec(memory_space=pltpu.VMEM)
    hbm = pl.BlockSpec(memory_space=pl.ANY)
    sem = pltpu.SemaphoreType.DMA
    lines = workers // 2
    bf16 = jnp.bfloat16
    result = pl.pallas_call(
        functools.partial(fused_kernel, workers, replicas),
        out_shape=jax.ShapeDtypeStruct((blocks, share, order), bf16),
        in_specs=[smem] * 2 + [vmem] * 7,
        out_specs=hbm,
        scratch_shapes=[
            pltpu.VMEM((2, replicas) + output_stats.shape[1:], bf16),
            pltpu.VMEM((2, workers, order, order), bf16),
            pltpu.VMEM((blocks, order, cols), bf16),
            pltpu.VMEM((blocks, share, order), bf16),
            pltpu.VMEM((blocks, share, order), bf16),
            sem((2, replicas - 1)),
            sem((2, replicas - 1)),
            sem((2, lines - 1)),
            sem((2, lines - 1)),
            sem((2, lines)),
            sem((2, lines)),
            sem((2, workers)),
            sem((2, workers)),
            sem((workers, replicas - 1)),
            sem((workers, replicas - 1)),
            sem((workers,)),
        ],
        compiler_params=pltpu.CompilerParams(
            collective_id=0, has_side_effects=True, vmem_limit_bytes=50 * 1024 * 1024
        ),
    )(
        first,
        second,
        gradients,
        output_stats,
        input_stats,
        output_factor,
        output_inverse,
        input_factor,
        input_inverse,
    )
    return pl.pallas_call(
        permute_kernel,
        out_shape=jax.ShapeDtypeStruct((blocks, share, order), bf16),
        in_specs=[smem, hbm],
        out_specs=hbm,
        scratch_shapes=[sem((blocks,))],
    )(slot[1], result)


def solution(mesh):
    in_specs = (
        P("work", None, "rep"),
        P("work", "rep", None),
        P("work", "rep", None),
        P("work", None, None),
        P("work", None, None),
        P("work", None, None),
        P("work", None, None),
        P(),
        P(),
        P(),
        P(),
    )
    out_specs = P("work", "rep", None)
    workers, replicas = mesh.shape["work"], mesh.shape["rep"]
    small = 4 <= workers <= 8 and replicas in (2, 4)
    local = gather_factors if small else exchange_blocks
    return jax.shard_map(local, mesh=mesh, in_specs=in_specs, out_specs=out_specs, check_vma=False)
```

```python
import functools

import jax
import jax.numpy as jnp
from jax import lax
from jax.experimental import pallas as pl
from jax.experimental.pallas import tpu as pltpu
from jax.sharding import PartitionSpec as P

decay_rate = 0.5


def refine(factor, inverse, samples):
    moment = jnp.dot(samples.T, samples, preferred_element_type=jnp.float32)
    updated = decay_rate * factor + (1.0 - decay_rate) / samples.shape[0] * moment
    product = jnp.dot(updated, inverse, precision=lax.Precision.HIGHEST)
    refined = 2.0 * inverse - jnp.dot(inverse, product, precision=lax.Precision.HIGHEST)
    return refined.astype(jnp.bfloat16)


def lookup(labels, values):
    matches = labels[:, None] == jnp.arange(values.shape[0], dtype=jnp.int32)[None, :]
    return jnp.sum(jnp.where(matches, values[None, :], 0), axis=1)


def group_rank(grouping):
    count = grouping.shape[0]
    positions = jnp.arange(count, dtype=jnp.int32)
    same_group = grouping[:, None] == grouping[None, :]
    earlier = positions[None, :] < positions[:, None]
    return jnp.sum(jnp.logical_and(same_group, earlier), axis=1)


def place_rows(target, data, out_count):
    selector = (jnp.arange(out_count, dtype=jnp.int32)[:, None] == target[None, :]).astype(
        jnp.bfloat16
    )
    return jnp.einsum("st,tij->sij", selector, data, preferred_element_type=jnp.float32).astype(
        jnp.bfloat16
    )


def pick_rows(source, data):
    selector = (source[:, None] == jnp.arange(data.shape[0], dtype=jnp.int32)[None, :]).astype(
        jnp.bfloat16
    )
    return jnp.einsum("st,tij->sij", selector, data, preferred_element_type=jnp.float32).astype(
        jnp.bfloat16
    )


def redirect(slot_count, holding, source_slot, target_slot):
    chosen = jnp.where(holding, source_slot, slot_count)
    return jnp.full((slot_count,), slot_count, jnp.int32).at[chosen].set(target_slot, mode="drop")


def relocate(buffer, target, slot_count):
    flat_view = buffer.reshape((slot_count,) + buffer.shape[2:])
    placed = place_rows(target, flat_view, slot_count)
    return placed.reshape(buffer.shape)


def exchange_blocks(
    gradients,
    output_stats,
    input_stats,
    output_factor,
    output_inverse,
    input_factor,
    input_inverse,
    block_output,
    block_input,
    output_owner,
    input_owner,
):
    workers = lax.axis_size("work")
    local_blocks, block_order, shard_cols = gradients.shape
    total_blocks = block_output.shape[0]
    capacity = (local_blocks + workers - 1) // workers
    slot_count = workers * capacity
    worker_index = lax.axis_index("work")
    home_index = jnp.arange(total_blocks, dtype=jnp.int32) // local_blocks
    out_dest = lookup(block_output, output_owner)
    in_dest = lookup(block_input, input_owner)
    first_rank = group_rank(home_index * workers + out_dest)
    second_rank = group_rank(out_dest * workers + in_dest)
    third_rank = group_rank(in_dest * workers + home_index)
    gathered_out, gathered_in = (
        lax.all_gather(output_stats, "rep", axis=1, tiled=True),
        lax.all_gather(input_stats, "rep", axis=1, tiled=True),
    )
    left_inverse = refine(output_factor[0], output_inverse[0], gathered_out[0])
    right_inverse = refine(input_factor[0], input_inverse[0], gathered_in[0])
    own_places = lax.dynamic_slice_in_dim(
        out_dest * capacity + first_rank, worker_index * local_blocks, local_blocks
    )
    outgoing = place_rows(own_places, gradients, slot_count)
    outgoing = outgoing.reshape(workers, capacity, block_order, shard_cols)
    arrived = jnp.einsum(
        "ij,nkjc->nkic",
        left_inverse,
        lax.all_to_all(outgoing, "work", split_axis=0, concat_axis=0, tiled=True),
        preferred_element_type=jnp.float32,
    ).astype(jnp.bfloat16)
    second_target = redirect(
        slot_count,
        out_dest == worker_index,
        home_index * capacity + first_rank,
        in_dest * capacity + second_rank,
    )
    forward = relocate(arrived, second_target, slot_count)
    third_target = redirect(
        slot_count,
        in_dest == worker_index,
        out_dest * capacity + second_rank,
        home_index * capacity + third_rank,
    )
    rows_form = lax.all_to_all(forward, "rep", split_axis=2, concat_axis=3, tiled=True)
    finished = jnp.einsum(
        "nkrc,cd->nkrd",
        lax.all_to_all(rows_form, "work", split_axis=0, concat_axis=0, tiled=True),
        right_inverse,
        preferred_element_type=jnp.float32,
    ).astype(jnp.bfloat16)
    backward = relocate(finished, third_target, slot_count)
    returned = lax.all_to_all(backward, "work", split_axis=0, concat_axis=0, tiled=True)
    returned = returned.reshape((slot_count,) + returned.shape[2:])
    own_slots = lax.dynamic_slice_in_dim(
        in_dest * capacity + third_rank, worker_index * local_blocks, local_blocks
    )
    return pick_rows(own_slots, returned)


def flip(value, mask):
    result, bit = value, 1
    while bit <= mask:
        if mask & bit:
            result = result + bit - 2 * bit * ((value // bit) % 2)
        bit *= 2
    return result


def halves(x):
    high = x.astype(jnp.bfloat16)
    return high, (x - high.astype(jnp.float32)).astype(jnp.bfloat16)


def dot(a, b):
    return jnp.dot(a, b, preferred_element_type=jnp.float32)


def exact_dot(a, b):
    return dot(a[0], b[0]) + (dot(a[0], b[1]) + dot(a[1], b[0]))


def fused_kernel(
    workers,
    replicas,
    first_ref,
    second_ref,
    g_hbm,
    os_ref,
    is_ref,
    of_hbm,
    oi_hbm,
    if_hbm,
    ii_hbm,
    out_ref,
    g_ref,
    of_ref,
    oi_ref,
    if_ref,
    ii_ref,
    stats,
    factors,
    middle,
    rows,
    result,
    stat_send,
    stat_recv,
    z_send,
    z_recv,
    y_send,
    y_recv,
    s_send,
    s_recv,
    m_send,
    m_recv,
    out_sem,
    load_sem,
):
    work, rep = lax.axis_index("work"), lax.axis_index("rep")
    blocks, order, cols = g_ref.shape
    capacity = blocks // workers
    lines = workers // 2
    share = order // replicas
    half = order // 2
    core = rep % 2
    sibling = {"rep": flip(rep, 1)}
    pending = []

    sources = (of_hbm, oi_hbm, if_hbm, ii_hbm, g_hbm)
    targets = (of_ref, oi_ref, if_ref, ii_ref, g_ref)
    loads = []
    for n, (source, target) in enumerate(zip(sources, targets)):
        loads.append(pltpu.make_async_copy(source, target, load_sem.at[n]))
        loads[n].start()

    barrier = pltpu.get_barrier_semaphore()
    peers = [{"rep": flip(rep, d)} for d in range(1, replicas)]
    peers += [{"work": flip(work, 1)}] + [{"work": flip(work, 2 * d)} for d in range(1, lines)]
    for peer in peers:
        pl.semaphore_signal(barrier, inc=1, device_id=peer, device_id_type=pl.DeviceIdType.MESH)
    pl.semaphore_wait(barrier, len(peers))

    def push(src, dst, send, recv, peer):
        copy = pltpu.make_async_remote_copy(
            src_ref=src,
            dst_ref=dst,
            send_sem=send,
            recv_sem=recv,
            device_id=peer,
            device_id_type=pl.DeviceIdType.MESH,
        )
        copy.start()
        pending.append(copy)
        return copy

    stat_copies = []
    for t, ref in enumerate((os_ref, is_ref)):
        for d in range(1, replicas):
            stat_copies.append(
                push(
                    ref.at[0],
                    stats.at[t, rep],
                    stat_send.at[t, d - 1],
                    stat_recv.at[t, d - 1],
                    {"rep": flip(rep, d)},
                )
            )
        stats[t, rep] = ref[0]

    mine = pl.ds(pl.multiple_of(core * half, half), half)
    places = [flip(work, i) for i in range(workers)]

    def chunk(t, i):
        return factors.at[t, places[i], mine]

    def refine_half(t, f_ref, i_ref):
        for copy in stat_copies[t * (replicas - 1) : (t + 1) * (replicas - 1)]:
            copy.wait_recv()
        loads[2 * t].wait()
        loads[2 * t + 1].wait()
        sample = stats[t].reshape(-1, order)
        moment = lax.dot_general(
            sample, sample, (((0,), (0,)), ((), ())), preferred_element_type=jnp.float32
        )
        updated = decay_rate * f_ref[0] + (1.0 - decay_rate) / sample.shape[0] * moment
        own = i_ref[0, mine]
        product = exact_dot(halves(own), halves(updated))
        refined = 2.0 * own - exact_dot(halves(product), halves(i_ref[0]))
        factors[t, places[0], mine] = refined.astype(jnp.bfloat16)

    z_copies, y_copies, s_copies = {}, {}, {}

    def to_sibling(t, i):
        s_copies[t, i] = push(chunk(t, i), chunk(t, i), s_send.at[t, i], s_recv.at[t, i], sibling)

    def to_y(t, d):
        y_copies[t, d] = push(
            chunk(t, 2 * d),
            chunk(t, 2 * d),
            y_send.at[t, d],
            y_recv.at[t, d],
            {"work": places[1]},
        )

    def to_z(t):
        for d in range(1, lines):
            z_copies[t, d] = push(
                chunk(t, 0),
                chunk(t, 0),
                z_send.at[t, d - 1],
                z_recv.at[t, d - 1],
                {"work": places[2 * d]},
            )

    m_copies = []
    own_cols = pl.ds(pl.multiple_of(rep * cols, cols), cols)
    own_rows = pl.ds(pl.multiple_of(rep * share, share), share)

    def left_multiply(i):
        slots = pl.ds(i * capacity, capacity)
        wide = jnp.concatenate(
            [g_ref[first_ref[i * capacity + k]] for k in range(capacity)], axis=1
        )
        for j in range(2):
            part = pl.ds(j * half, half)
            product = dot(factors[0, places[i], part], wide).astype(jnp.bfloat16)
            for k in range(capacity):
                middle[i * capacity + k, part] = product[:, k * cols : (k + 1) * cols]
        for d in range(replicas - 1, 0, -1):
            other = flip(rep, d)
            m_copies.append(
                push(
                    middle.at[slots, pl.ds(pl.multiple_of(other * share, share), share)],
                    rows.at[slots, :, own_cols],
                    m_send.at[i, d - 1],
                    m_recv.at[i, d - 1],
                    {"rep": other},
                )
            )
        rows[slots, :, own_cols] = middle[slots, own_rows]

    def spread(t, ready):
        queue = []
        for d in range(1, lines + 1):
            if d < lines:
                z_copies[t, d].wait_recv()
                to_y(t, d)
                to_sibling(t, 2 * d)
                if d == lines - 1 and t == 0:
                    to_y(1, 0)
                    to_z(1)
                    to_sibling(1, 0)
            while queue:
                i = queue.pop(0)
                s_copies[t, i].wait_recv()
                ready(i)
            y_copies[t, d - 1].wait_recv()
            to_sibling(t, 2 * d - 1)
            if d < lines:
                queue.append(2 * d)
            queue.append(2 * d - 1)
        for i in queue:
            s_copies[t, i].wait_recv()
            ready(i)

    refine_half(0, of_ref, oi_ref)
    to_y(0, 0)
    to_z(0)
    to_sibling(0, 0)
    loads[4].wait()
    s_copies[0, 0].wait_recv()
    left_multiply(0)
    refine_half(1, if_ref, ii_ref)
    spread(0, left_multiply)
    s_copies[1, 0].wait_recv()
    spread(1, lambda i: None)
    for copy in m_copies:
        copy.wait_recv()
    out_copies = []
    for i in range(workers):
        slots = pl.ds(i * capacity, capacity)
        for k in range(0, capacity, 2):
            pair = [rows[second_ref[i * capacity + k + j]] for j in range(min(2, capacity - k))]
            product = dot(jnp.concatenate(pair, axis=0), factors[1, places[i]])
            for j in range(len(pair)):
                result[i * capacity + k + j] = product[j * share : (j + 1) * share].astype(
                    jnp.bfloat16
                )
        copy = pltpu.make_async_copy(result.at[slots], out_ref.at[slots], out_sem.at[i])
        copy.start()
        out_copies.append(copy)
    for copy in out_copies:
        copy.wait()
    for copy in pending:
        copy.wait_send()


def permute_kernel(place_ref, in_ref, out_ref, buffer, in_sems, out_sems):
    blocks = in_ref.shape[0]
    loads = []
    for b in range(blocks):
        loads.append(
            pltpu.make_async_copy(in_ref.at[place_ref[b]], buffer.at[b], in_sems.at[b])
        )
        loads[b].start()
    stores = []
    for b in range(blocks):
        loads[b].wait()
        stores.append(pltpu.make_async_copy(buffer.at[b], out_ref.at[b], out_sems.at[b]))
        stores[b].start()
    for copy in stores:
        copy.wait()


def gather_factors(
    gradients,
    output_stats,
    input_stats,
    output_factor,
    output_inverse,
    input_factor,
    input_inverse,
    block_output,
    block_input,
    output_owner,
    input_owner,
):
    workers, replicas = lax.axis_size("work"), lax.axis_size("rep")
    blocks, order, cols = gradients.shape
    capacity = blocks // workers
    share = order // replicas
    work = lax.axis_index("work")
    at = jnp.arange(blocks, dtype=jnp.int32)

    def slots_of(labels, owner):
        labels = lax.dynamic_slice_in_dim(labels, work * blocks, blocks)
        dest = lookup(labels, owner ^ work)
        return dest * capacity + group_rank(dest)

    def by_slot(slot, values):
        return jnp.sum(jnp.where(slot[None, :] == at[:, None], values[None, :], 0), axis=1)

    out_slot = slots_of(block_output, output_owner)
    in_slot = slots_of(block_input, input_owner)
    first, second = by_slot(out_slot, at), by_slot(in_slot, out_slot)
    smem = pl.BlockSpec(memory_space=pltpu.SMEM)
    vmem = pl.BlockSpec(memory_space=pltpu.VMEM)
    hbm = pl.BlockSpec(memory_space=pl.ANY)
    sem = pltpu.SemaphoreType.DMA
    lines = workers // 2
    bf16 = jnp.bfloat16
    result = pl.pallas_call(
        functools.partial(fused_kernel, workers, replicas),
        out_shape=jax.ShapeDtypeStruct((blocks, share, order), bf16),
        in_specs=[smem] * 2 + [hbm] + [vmem] * 2 + [hbm] * 4,
        out_specs=hbm,
        scratch_shapes=[
            pltpu.VMEM(gradients.shape, bf16),
            pltpu.VMEM(output_factor.shape, jnp.float32),
            pltpu.VMEM(output_inverse.shape, jnp.float32),
            pltpu.VMEM(input_factor.shape, jnp.float32),
            pltpu.VMEM(input_inverse.shape, jnp.float32),
            pltpu.VMEM((2, replicas) + output_stats.shape[1:], bf16),
            pltpu.VMEM((2, workers, order, order), bf16),
            pltpu.VMEM((blocks, order, cols), bf16),
            pltpu.VMEM((blocks, share, order), bf16),
            pltpu.VMEM((blocks, share, order), bf16),
            sem((2, replicas - 1)),
            sem((2, replicas - 1)),
            sem((2, lines - 1)),
            sem((2, lines - 1)),
            sem((2, lines)),
            sem((2, lines)),
            sem((2, workers)),
            sem((2, workers)),
            sem((workers, replicas - 1)),
            sem((workers, replicas - 1)),
            sem((workers,)),
            sem((5,)),
        ],
        compiler_params=pltpu.CompilerParams(
            collective_id=0, has_side_effects=True, vmem_limit_bytes=58 * 1024 * 1024
        ),
    )(
        first,
        second,
        gradients,
        output_stats,
        input_stats,
        output_factor,
        output_inverse,
        input_factor,
        input_inverse,
    )
    return pl.pallas_call(
        permute_kernel,
        out_shape=jax.ShapeDtypeStruct((blocks, share, order), bf16),
        in_specs=[smem, hbm],
        out_specs=hbm,
        scratch_shapes=[
            pltpu.VMEM((blocks, share, order), bf16),
            sem((blocks,)),
            sem((blocks,)),
        ],
        compiler_params=pltpu.CompilerParams(vmem_limit_bytes=56 * 1024 * 1024),
    )(in_slot, result)


def solution(mesh):
    in_specs = (
        P("work", None, "rep"),
        P("work", "rep", None),
        P("work", "rep", None),
        P("work", None, None),
        P("work", None, None),
        P("work", None, None),
        P("work", None, None),
        P(),
        P(),
        P(),
        P(),
    )
    out_specs = P("work", "rep", None)
    workers, replicas = mesh.shape["work"], mesh.shape["rep"]
    small = 4 <= workers <= 8 and replicas in (2, 4)
    local = gather_factors if small else exchange_blocks
    return jax.shard_map(local, mesh=mesh, in_specs=in_specs, out_specs=out_specs, check_vma=False)
```

```python
import functools

import jax
import jax.numpy as jnp
from jax import lax
from jax.experimental import pallas as pl
from jax.experimental.pallas import tpu as pltpu
from jax.sharding import PartitionSpec as P

decay_rate = 0.5


def refine(factor, inverse, samples):
    moment = jnp.dot(samples.T, samples, preferred_element_type=jnp.float32)
    updated = decay_rate * factor + (1.0 - decay_rate) / samples.shape[0] * moment
    product = jnp.dot(updated, inverse, precision=lax.Precision.HIGHEST)
    refined = 2.0 * inverse - jnp.dot(inverse, product, precision=lax.Precision.HIGHEST)
    return refined.astype(jnp.bfloat16)


def lookup(labels, values):
    matches = labels[:, None] == jnp.arange(values.shape[0], dtype=jnp.int32)[None, :]
    return jnp.sum(jnp.where(matches, values[None, :], 0), axis=1)


def group_rank(grouping):
    count = grouping.shape[0]
    positions = jnp.arange(count, dtype=jnp.int32)
    same_group = grouping[:, None] == grouping[None, :]
    earlier = positions[None, :] < positions[:, None]
    return jnp.sum(jnp.logical_and(same_group, earlier), axis=1)


def place_rows(target, data, out_count):
    selector = (jnp.arange(out_count, dtype=jnp.int32)[:, None] == target[None, :]).astype(
        jnp.bfloat16
    )
    return jnp.einsum("st,tij->sij", selector, data, preferred_element_type=jnp.float32).astype(
        jnp.bfloat16
    )


def pick_rows(source, data):
    selector = (source[:, None] == jnp.arange(data.shape[0], dtype=jnp.int32)[None, :]).astype(
        jnp.bfloat16
    )
    return jnp.einsum("st,tij->sij", selector, data, preferred_element_type=jnp.float32).astype(
        jnp.bfloat16
    )


def redirect(slot_count, holding, source_slot, target_slot):
    chosen = jnp.where(holding, source_slot, slot_count)
    return jnp.full((slot_count,), slot_count, jnp.int32).at[chosen].set(target_slot, mode="drop")


def relocate(buffer, target, slot_count):
    flat_view = buffer.reshape((slot_count,) + buffer.shape[2:])
    placed = place_rows(target, flat_view, slot_count)
    return placed.reshape(buffer.shape)


def exchange_blocks(
    gradients,
    output_stats,
    input_stats,
    output_factor,
    output_inverse,
    input_factor,
    input_inverse,
    block_output,
    block_input,
    output_owner,
    input_owner,
):
    workers = lax.axis_size("work")
    local_blocks, block_order, shard_cols = gradients.shape
    total_blocks = block_output.shape[0]
    capacity = (local_blocks + workers - 1) // workers
    slot_count = workers * capacity
    worker_index = lax.axis_index("work")
    home_index = jnp.arange(total_blocks, dtype=jnp.int32) // local_blocks
    out_dest = lookup(block_output, output_owner)
    in_dest = lookup(block_input, input_owner)
    first_rank = group_rank(home_index * workers + out_dest)
    second_rank = group_rank(out_dest * workers + in_dest)
    third_rank = group_rank(in_dest * workers + home_index)
    gathered_out, gathered_in = (
        lax.all_gather(output_stats, "rep", axis=1, tiled=True),
        lax.all_gather(input_stats, "rep", axis=1, tiled=True),
    )
    left_inverse = refine(output_factor[0], output_inverse[0], gathered_out[0])
    right_inverse = refine(input_factor[0], input_inverse[0], gathered_in[0])
    own_places = lax.dynamic_slice_in_dim(
        out_dest * capacity + first_rank, worker_index * local_blocks, local_blocks
    )
    outgoing = place_rows(own_places, gradients, slot_count)
    outgoing = outgoing.reshape(workers, capacity, block_order, shard_cols)
    arrived = jnp.einsum(
        "ij,nkjc->nkic",
        left_inverse,
        lax.all_to_all(outgoing, "work", split_axis=0, concat_axis=0, tiled=True),
        preferred_element_type=jnp.float32,
    ).astype(jnp.bfloat16)
    second_target = redirect(
        slot_count,
        out_dest == worker_index,
        home_index * capacity + first_rank,
        in_dest * capacity + second_rank,
    )
    forward = relocate(arrived, second_target, slot_count)
    third_target = redirect(
        slot_count,
        in_dest == worker_index,
        out_dest * capacity + second_rank,
        home_index * capacity + third_rank,
    )
    rows_form = lax.all_to_all(forward, "rep", split_axis=2, concat_axis=3, tiled=True)
    finished = jnp.einsum(
        "nkrc,cd->nkrd",
        lax.all_to_all(rows_form, "work", split_axis=0, concat_axis=0, tiled=True),
        right_inverse,
        preferred_element_type=jnp.float32,
    ).astype(jnp.bfloat16)
    backward = relocate(finished, third_target, slot_count)
    returned = lax.all_to_all(backward, "work", split_axis=0, concat_axis=0, tiled=True)
    returned = returned.reshape((slot_count,) + returned.shape[2:])
    own_slots = lax.dynamic_slice_in_dim(
        in_dest * capacity + third_rank, worker_index * local_blocks, local_blocks
    )
    return pick_rows(own_slots, returned)


def flip(value, mask):
    result, bit = value, 1
    while bit <= mask:
        if mask & bit:
            result = result + bit - 2 * bit * ((value // bit) % 2)
        bit *= 2
    return result


def halves(x):
    high = x.astype(jnp.bfloat16)
    return high, (x - high.astype(jnp.float32)).astype(jnp.bfloat16)


def dot(a, b):
    return jnp.dot(a, b, preferred_element_type=jnp.float32)


def exact_dot(a, b):
    return dot(a[0], b[0]) + (dot(a[0], b[1]) + dot(a[1], b[0]))


def fused_kernel(
    workers,
    replicas,
    first_ref,
    second_ref,
    g_hbm,
    os_ref,
    is_ref,
    of_hbm,
    oi_hbm,
    if_hbm,
    ii_hbm,
    out_ref,
    g_ref,
    of_ref,
    oi_ref,
    if_ref,
    ii_ref,
    stats,
    factors,
    middle,
    rows,
    result,
    stat_send,
    stat_recv,
    z_send,
    z_recv,
    y_send,
    y_recv,
    s_send,
    s_recv,
    m_send,
    m_recv,
    out_sem,
    load_sem,
):
    work, rep = lax.axis_index("work"), lax.axis_index("rep")
    blocks, order, cols = g_ref.shape
    capacity = blocks // workers
    lines = workers // 2
    share = order // replicas
    half = order // 2
    core = rep % 2
    sibling = {"rep": flip(rep, 1)}
    pending = []

    sources = (of_hbm, oi_hbm, if_hbm, ii_hbm, g_hbm)
    targets = (of_ref, oi_ref, if_ref, ii_ref, g_ref)
    loads = []
    for n, (source, target) in enumerate(zip(sources, targets)):
        loads.append(pltpu.make_async_copy(source, target, load_sem.at[n]))
        loads[n].start()

    barrier = pltpu.get_barrier_semaphore()
    peers = [{"rep": flip(rep, d)} for d in range(1, replicas)]
    peers += [{"work": flip(work, 1)}] + [{"work": flip(work, 2 * d)} for d in range(1, lines)]
    for peer in peers:
        pl.semaphore_signal(barrier, inc=1, device_id=peer, device_id_type=pl.DeviceIdType.MESH)
    pl.semaphore_wait(barrier, len(peers))

    def push(src, dst, send, recv, peer):
        copy = pltpu.make_async_remote_copy(
            src_ref=src,
            dst_ref=dst,
            send_sem=send,
            recv_sem=recv,
            device_id=peer,
            device_id_type=pl.DeviceIdType.MESH,
        )
        copy.start()
        pending.append(copy)
        return copy

    stat_copies = []
    for t, ref in enumerate((os_ref, is_ref)):
        for d in range(1, replicas):
            stat_copies.append(
                push(
                    ref.at[0],
                    stats.at[t, rep],
                    stat_send.at[t, d - 1],
                    stat_recv.at[t, d - 1],
                    {"rep": flip(rep, d)},
                )
            )
        stats[t, rep] = ref[0]

    mine = pl.ds(pl.multiple_of(core * half, half), half)
    places = [flip(work, i) for i in range(workers)]

    def chunk(t, i):
        return factors.at[t, places[i], mine]

    def refine_half(t, f_ref, i_ref):
        for copy in stat_copies[t * (replicas - 1) : (t + 1) * (replicas - 1)]:
            copy.wait_recv()
        loads[2 * t].wait()
        loads[2 * t + 1].wait()
        sample = stats[t].reshape(-1, order)
        moment = lax.dot_general(
            sample, sample, (((0,), (0,)), ((), ())), preferred_element_type=jnp.float32
        )
        updated = decay_rate * f_ref[0] + (1.0 - decay_rate) / sample.shape[0] * moment
        own = i_ref[0, mine]
        product = exact_dot(halves(own), halves(updated))
        refined = 2.0 * own - exact_dot(halves(product), halves(i_ref[0]))
        factors[t, places[0], mine] = refined.astype(jnp.bfloat16)

    z_copies, y_copies, s_copies = {}, {}, {}

    def to_sibling(t, i):
        s_copies[t, i] = push(chunk(t, i), chunk(t, i), s_send.at[t, i], s_recv.at[t, i], sibling)

    def to_y(t, d):
        y_copies[t, d] = push(
            chunk(t, 2 * d),
            chunk(t, 2 * d),
            y_send.at[t, d],
            y_recv.at[t, d],
            {"work": places[1]},
        )

    def to_z(t):
        for d in range(1, lines):
            z_copies[t, d] = push(
                chunk(t, 0),
                chunk(t, 0),
                z_send.at[t, d - 1],
                z_recv.at[t, d - 1],
                {"work": places[2 * d]},
            )

    m_copies = []
    own_cols = pl.ds(pl.multiple_of(rep * cols, cols), cols)
    own_rows = pl.ds(pl.multiple_of(rep * share, share), share)

    def left_multiply(i):
        slots = pl.ds(i * capacity, capacity)
        wide = jnp.concatenate(
            [g_ref[first_ref[i * capacity + k]] for k in range(capacity)], axis=1
        )
        for j in range(2):
            part = pl.ds(j * half, half)
            product = dot(factors[0, places[i], part], wide).astype(jnp.bfloat16)
            for k in range(capacity):
                middle[i * capacity + k, part] = product[:, k * cols : (k + 1) * cols]
        for d in range(replicas - 1, 0, -1):
            other = flip(rep, d)
            m_copies.append(
                push(
                    middle.at[slots, pl.ds(pl.multiple_of(other * share, share), share)],
                    rows.at[slots, :, own_cols],
                    m_send.at[i, d - 1],
                    m_recv.at[i, d - 1],
                    {"rep": other},
                )
            )
        rows[slots, :, own_cols] = middle[slots, own_rows]

    def spread_left(t, ready):
        queue = []
        for d in range(1, lines + 1):
            if d < lines:
                z_copies[t, d].wait_recv()
                to_y(t, d)
                to_sibling(t, 2 * d)
                if d == 1:
                    to_y(1, 0)
                    to_sibling(1, 0)
                if d == lines // 2:
                    to_z(1)
            while queue:
                i = queue.pop(0)
                s_copies[t, i].wait_recv()
                ready(i)
            y_copies[t, d - 1].wait_recv()
            to_sibling(t, 2 * d - 1)
            if d < lines:
                queue.append(2 * d)
            queue.append(2 * d - 1)
        for i in queue:
            s_copies[t, i].wait_recv()
            ready(i)

    def spread_right(t):
        for d in range(1, lines):
            z_copies[t, d].wait_recv()
            to_y(t, d)
            to_sibling(t, 2 * d)
        for d in range(lines):
            y_copies[t, d].wait_recv()
            to_sibling(t, 2 * d + 1)
        for i in range(workers):
            s_copies[t, i].wait_recv()

    refine_half(0, of_ref, oi_ref)
    to_y(0, 0)
    to_z(0)
    to_sibling(0, 0)
    loads[4].wait()
    s_copies[0, 0].wait_recv()
    left_multiply(0)
    refine_half(1, if_ref, ii_ref)
    spread_left(0, left_multiply)
    spread_right(1)
    for copy in m_copies:
        copy.wait_recv()
    out_copies = []
    for i in range(workers):
        slots = pl.ds(i * capacity, capacity)
        for k in range(0, capacity, 2):
            pair = [rows[second_ref[i * capacity + k + j]] for j in range(min(2, capacity - k))]
            product = dot(jnp.concatenate(pair, axis=0), factors[1, places[i]])
            for j in range(len(pair)):
                result[i * capacity + k + j] = product[j * share : (j + 1) * share].astype(
                    jnp.bfloat16
                )
        copy = pltpu.make_async_copy(result.at[slots], out_ref.at[slots], out_sem.at[i])
        copy.start()
        out_copies.append(copy)
    for copy in out_copies:
        copy.wait()
    for copy in pending:
        copy.wait_send()


def permute_kernel(place_ref, in_ref, out_ref, buffer, in_sems, out_sems):
    blocks = in_ref.shape[0]
    loads = []
    for b in range(blocks):
        loads.append(
            pltpu.make_async_copy(in_ref.at[place_ref[b]], buffer.at[b], in_sems.at[b])
        )
        loads[b].start()
    stores = []
    for b in range(blocks):
        loads[b].wait()
        stores.append(pltpu.make_async_copy(buffer.at[b], out_ref.at[b], out_sems.at[b]))
        stores[b].start()
    for copy in stores:
        copy.wait()


def gather_factors(
    gradients,
    output_stats,
    input_stats,
    output_factor,
    output_inverse,
    input_factor,
    input_inverse,
    block_output,
    block_input,
    output_owner,
    input_owner,
):
    workers, replicas = lax.axis_size("work"), lax.axis_size("rep")
    blocks, order, cols = gradients.shape
    capacity = blocks // workers
    share = order // replicas
    work = lax.axis_index("work")
    at = jnp.arange(blocks, dtype=jnp.int32)

    def slots_of(labels, owner):
        labels = lax.dynamic_slice_in_dim(labels, work * blocks, blocks)
        dest = lookup(labels, owner ^ work)
        return dest * capacity + group_rank(dest)

    def by_slot(slot, values):
        return jnp.sum(jnp.where(slot[None, :] == at[:, None], values[None, :], 0), axis=1)

    out_slot = slots_of(block_output, output_owner)
    in_slot = slots_of(block_input, input_owner)
    first, second = by_slot(out_slot, at), by_slot(in_slot, out_slot)
    smem = pl.BlockSpec(memory_space=pltpu.SMEM)
    vmem = pl.BlockSpec(memory_space=pltpu.VMEM)
    hbm = pl.BlockSpec(memory_space=pl.ANY)
    sem = pltpu.SemaphoreType.DMA
    lines = workers // 2
    bf16 = jnp.bfloat16
    result = pl.pallas_call(
        functools.partial(fused_kernel, workers, replicas),
        out_shape=jax.ShapeDtypeStruct((blocks, share, order), bf16),
        in_specs=[smem] * 2 + [hbm] + [vmem] * 2 + [hbm] * 4,
        out_specs=hbm,
        scratch_shapes=[
            pltpu.VMEM(gradients.shape, bf16),
            pltpu.VMEM(output_factor.shape, jnp.float32),
            pltpu.VMEM(output_inverse.shape, jnp.float32),
            pltpu.VMEM(input_factor.shape, jnp.float32),
            pltpu.VMEM(input_inverse.shape, jnp.float32),
            pltpu.VMEM((2, replicas) + output_stats.shape[1:], bf16),
            pltpu.VMEM((2, workers, order, order), bf16),
            pltpu.VMEM((blocks, order, cols), bf16),
            pltpu.VMEM((blocks, share, order), bf16),
            pltpu.VMEM((blocks, share, order), bf16),
            sem((2, replicas - 1)),
            sem((2, replicas - 1)),
            sem((2, lines - 1)),
            sem((2, lines - 1)),
            sem((2, lines)),
            sem((2, lines)),
            sem((2, workers)),
            sem((2, workers)),
            sem((workers, replicas - 1)),
            sem((workers, replicas - 1)),
            sem((workers,)),
            sem((5,)),
        ],
        compiler_params=pltpu.CompilerParams(
            collective_id=0, has_side_effects=True, vmem_limit_bytes=58 * 1024 * 1024
        ),
    )(
        first,
        second,
        gradients,
        output_stats,
        input_stats,
        output_factor,
        output_inverse,
        input_factor,
        input_inverse,
    )
    return pl.pallas_call(
        permute_kernel,
        out_shape=jax.ShapeDtypeStruct((blocks, share, order), bf16),
        in_specs=[smem, hbm],
        out_specs=hbm,
        scratch_shapes=[
            pltpu.VMEM((blocks, share, order), bf16),
            sem((blocks,)),
            sem((blocks,)),
        ],
        compiler_params=pltpu.CompilerParams(vmem_limit_bytes=56 * 1024 * 1024),
    )(in_slot, result)


def solution(mesh):
    in_specs = (
        P("work", None, "rep"),
        P("work", "rep", None),
        P("work", "rep", None),
        P("work", None, None),
        P("work", None, None),
        P("work", None, None),
        P("work", None, None),
        P(),
        P(),
        P(),
        P(),
    )
    out_specs = P("work", "rep", None)
    workers, replicas = mesh.shape["work"], mesh.shape["rep"]
    small = 4 <= workers <= 8 and replicas in (2, 4)
    local = gather_factors if small else exchange_blocks
    return jax.shard_map(local, mesh=mesh, in_specs=in_specs, out_specs=out_specs, check_vma=False)
```

```python
import functools

import jax
import jax.numpy as jnp
from jax import lax
from jax.experimental import pallas as pl
from jax.experimental.pallas import tpu as pltpu
from jax.sharding import PartitionSpec as P

decay_rate = 0.5


def refine(factor, inverse, samples):
    moment = jnp.dot(samples.T, samples, preferred_element_type=jnp.float32)
    updated = decay_rate * factor + (1.0 - decay_rate) / samples.shape[0] * moment
    product = jnp.dot(updated, inverse, precision=lax.Precision.HIGHEST)
    refined = 2.0 * inverse - jnp.dot(inverse, product, precision=lax.Precision.HIGHEST)
    return refined.astype(jnp.bfloat16)


def lookup(labels, values):
    matches = labels[:, None] == jnp.arange(values.shape[0], dtype=jnp.int32)[None, :]
    return jnp.sum(jnp.where(matches, values[None, :], 0), axis=1)


def group_rank(grouping):
    count = grouping.shape[0]
    positions = jnp.arange(count, dtype=jnp.int32)
    same_group = grouping[:, None] == grouping[None, :]
    earlier = positions[None, :] < positions[:, None]
    return jnp.sum(jnp.logical_and(same_group, earlier), axis=1)


def place_rows(target, data, out_count):
    selector = (jnp.arange(out_count, dtype=jnp.int32)[:, None] == target[None, :]).astype(
        jnp.bfloat16
    )
    return jnp.einsum("st,tij->sij", selector, data, preferred_element_type=jnp.float32).astype(
        jnp.bfloat16
    )


def pick_rows(source, data):
    selector = (source[:, None] == jnp.arange(data.shape[0], dtype=jnp.int32)[None, :]).astype(
        jnp.bfloat16
    )
    return jnp.einsum("st,tij->sij", selector, data, preferred_element_type=jnp.float32).astype(
        jnp.bfloat16
    )


def redirect(slot_count, holding, source_slot, target_slot):
    chosen = jnp.where(holding, source_slot, slot_count)
    return jnp.full((slot_count,), slot_count, jnp.int32).at[chosen].set(target_slot, mode="drop")


def relocate(buffer, target, slot_count):
    flat_view = buffer.reshape((slot_count,) + buffer.shape[2:])
    placed = place_rows(target, flat_view, slot_count)
    return placed.reshape(buffer.shape)


def exchange_blocks(
    gradients,
    output_stats,
    input_stats,
    output_factor,
    output_inverse,
    input_factor,
    input_inverse,
    block_output,
    block_input,
    output_owner,
    input_owner,
):
    workers = lax.axis_size("work")
    local_blocks, block_order, shard_cols = gradients.shape
    total_blocks = block_output.shape[0]
    capacity = (local_blocks + workers - 1) // workers
    slot_count = workers * capacity
    worker_index = lax.axis_index("work")
    home_index = jnp.arange(total_blocks, dtype=jnp.int32) // local_blocks
    out_dest = lookup(block_output, output_owner)
    in_dest = lookup(block_input, input_owner)
    first_rank = group_rank(home_index * workers + out_dest)
    second_rank = group_rank(out_dest * workers + in_dest)
    third_rank = group_rank(in_dest * workers + home_index)
    gathered_out, gathered_in = (
        lax.all_gather(output_stats, "rep", axis=1, tiled=True),
        lax.all_gather(input_stats, "rep", axis=1, tiled=True),
    )
    left_inverse = refine(output_factor[0], output_inverse[0], gathered_out[0])
    right_inverse = refine(input_factor[0], input_inverse[0], gathered_in[0])
    own_places = lax.dynamic_slice_in_dim(
        out_dest * capacity + first_rank, worker_index * local_blocks, local_blocks
    )
    outgoing = place_rows(own_places, gradients, slot_count)
    outgoing = outgoing.reshape(workers, capacity, block_order, shard_cols)
    arrived = jnp.einsum(
        "ij,nkjc->nkic",
        left_inverse,
        lax.all_to_all(outgoing, "work", split_axis=0, concat_axis=0, tiled=True),
        preferred_element_type=jnp.float32,
    ).astype(jnp.bfloat16)
    second_target = redirect(
        slot_count,
        out_dest == worker_index,
        home_index * capacity + first_rank,
        in_dest * capacity + second_rank,
    )
    forward = relocate(arrived, second_target, slot_count)
    third_target = redirect(
        slot_count,
        in_dest == worker_index,
        out_dest * capacity + second_rank,
        home_index * capacity + third_rank,
    )
    rows_form = lax.all_to_all(forward, "rep", split_axis=2, concat_axis=3, tiled=True)
    finished = jnp.einsum(
        "nkrc,cd->nkrd",
        lax.all_to_all(rows_form, "work", split_axis=0, concat_axis=0, tiled=True),
        right_inverse,
        preferred_element_type=jnp.float32,
    ).astype(jnp.bfloat16)
    backward = relocate(finished, third_target, slot_count)
    returned = lax.all_to_all(backward, "work", split_axis=0, concat_axis=0, tiled=True)
    returned = returned.reshape((slot_count,) + returned.shape[2:])
    own_slots = lax.dynamic_slice_in_dim(
        in_dest * capacity + third_rank, worker_index * local_blocks, local_blocks
    )
    return pick_rows(own_slots, returned)


def flip(value, mask):
    result, bit = value, 1
    while bit <= mask:
        if mask & bit:
            result = result + bit - 2 * bit * ((value // bit) % 2)
        bit *= 2
    return result


def halves(x):
    high = x.astype(jnp.bfloat16)
    return high, (x - high.astype(jnp.float32)).astype(jnp.bfloat16)


def dot(a, b):
    return jnp.dot(a, b, preferred_element_type=jnp.float32)


def exact_dot(a, b):
    return dot(a[0], b[0]) + (dot(a[0], b[1]) + dot(a[1], b[0]))


def fused_kernel(
    workers,
    replicas,
    first_ref,
    second_ref,
    g_hbm,
    os_ref,
    is_ref,
    of_hbm,
    oi_hbm,
    if_hbm,
    ii_hbm,
    out_ref,
    g_ref,
    of_ref,
    oi_ref,
    if_ref,
    ii_ref,
    stats,
    factors,
    middle,
    rows,
    result,
    stat_send,
    stat_recv,
    z_send,
    z_recv,
    y_send,
    y_recv,
    s_send,
    s_recv,
    m_send,
    m_recv,
    out_sem,
    load_sem,
):
    work, rep = lax.axis_index("work"), lax.axis_index("rep")
    blocks, order, cols = g_ref.shape
    capacity = blocks // workers
    lines = workers // 2
    share = order // replicas
    half = order // 2
    core = rep % 2
    sibling = {"rep": flip(rep, 1)}
    pending = []

    sources = (of_hbm, oi_hbm, if_hbm, ii_hbm, g_hbm)
    targets = (of_ref, oi_ref, if_ref, ii_ref, g_ref)
    loads = []
    for n, (source, target) in enumerate(zip(sources, targets)):
        loads.append(pltpu.make_async_copy(source, target, load_sem.at[n]))
        loads[n].start()

    barrier = pltpu.get_barrier_semaphore()
    peers = [{"rep": flip(rep, d)} for d in range(1, replicas)]
    peers += [{"work": flip(work, 1)}] + [{"work": flip(work, 2 * d)} for d in range(1, lines)]
    for peer in peers:
        pl.semaphore_signal(barrier, inc=1, device_id=peer, device_id_type=pl.DeviceIdType.MESH)
    pl.semaphore_wait(barrier, len(peers))

    def push(src, dst, send, recv, peer):
        copy = pltpu.make_async_remote_copy(
            src_ref=src,
            dst_ref=dst,
            send_sem=send,
            recv_sem=recv,
            device_id=peer,
            device_id_type=pl.DeviceIdType.MESH,
        )
        copy.start()
        pending.append(copy)
        return copy

    stat_copies = []
    for t, ref in enumerate((os_ref, is_ref)):
        for d in range(1, replicas):
            stat_copies.append(
                push(
                    ref.at[0],
                    stats.at[t, rep],
                    stat_send.at[t, d - 1],
                    stat_recv.at[t, d - 1],
                    {"rep": flip(rep, d)},
                )
            )
        stats[t, rep] = ref[0]

    mine = pl.ds(pl.multiple_of(core * half, half), half)
    places = [flip(work, i) for i in range(workers)]

    def chunk(t, i):
        return factors.at[t, places[i], mine]

    def refine_half(t, f_ref, i_ref):
        for copy in stat_copies[t * (replicas - 1) : (t + 1) * (replicas - 1)]:
            copy.wait_recv()
        loads[2 * t].wait()
        loads[2 * t + 1].wait()
        sample = stats[t].reshape(-1, order)
        moment = lax.dot_general(
            sample, sample, (((0,), (0,)), ((), ())), preferred_element_type=jnp.float32
        )
        updated = decay_rate * f_ref[0] + (1.0 - decay_rate) / sample.shape[0] * moment
        own = i_ref[0, mine]
        product = exact_dot(halves(own), halves(updated))
        refined = 2.0 * own - exact_dot(halves(product), halves(i_ref[0]))
        factors[t, places[0], mine] = refined.astype(jnp.bfloat16)

    z_copies, y_copies, s_copies = {}, {}, {}

    def to_sibling(t, i):
        s_copies[t, i] = push(chunk(t, i), chunk(t, i), s_send.at[t, i], s_recv.at[t, i], sibling)

    def to_y(t, d):
        y_copies[t, d] = push(
            chunk(t, 2 * d),
            chunk(t, 2 * d),
            y_send.at[t, d],
            y_recv.at[t, d],
            {"work": places[1]},
        )

    def to_z(t):
        for d in range(1, lines):
            z_copies[t, d] = push(
                chunk(t, 0),
                chunk(t, 0),
                z_send.at[t, d - 1],
                z_recv.at[t, d - 1],
                {"work": places[2 * d]},
            )

    m_copies = []
    own_rows = pl.ds(pl.multiple_of(rep * share, share), share)

    def left_multiply(i):
        slots = pl.ds(i * capacity, capacity)
        wide = jnp.concatenate(
            [g_ref[first_ref[i * capacity + k]] for k in range(capacity)], axis=1
        )
        for j in range(2):
            part = pl.ds(j * half, half)
            product = dot(factors[0, places[i], part], wide).astype(jnp.bfloat16)
            for k in range(capacity):
                middle[i * capacity + k, part] = product[:, k * cols : (k + 1) * cols]
        for d in range(replicas - 1, 0, -1):
            other = flip(rep, d)
            m_copies.append(
                push(
                    middle.at[slots, pl.ds(pl.multiple_of(other * share, share), share)],
                    rows.at[rep, slots],
                    m_send.at[i, d - 1],
                    m_recv.at[i, d - 1],
                    {"rep": other},
                )
            )
        rows[rep, slots] = middle[slots, own_rows]

    def spread(t, ready):
        queue = []
        for d in range(1, lines + 1):
            if d < lines:
                z_copies[t, d].wait_recv()
                to_y(t, d)
                to_sibling(t, 2 * d)
                if d == lines - 1 and t == 0:
                    to_y(1, 0)
                    to_z(1)
                    to_sibling(1, 0)
            while queue:
                i = queue.pop(0)
                s_copies[t, i].wait_recv()
                ready(i)
            y_copies[t, d - 1].wait_recv()
            to_sibling(t, 2 * d - 1)
            if d < lines:
                queue.append(2 * d)
            queue.append(2 * d - 1)
        for i in queue:
            s_copies[t, i].wait_recv()
            ready(i)

    refine_half(0, of_ref, oi_ref)
    to_y(0, 0)
    to_z(0)
    to_sibling(0, 0)
    loads[4].wait()
    s_copies[0, 0].wait_recv()
    left_multiply(0)
    refine_half(1, if_ref, ii_ref)
    spread(0, left_multiply)
    s_copies[1, 0].wait_recv()
    spread(1, lambda i: None)
    for copy in m_copies:
        copy.wait_recv()
    out_copies = []
    for i in range(workers):
        slots = pl.ds(i * capacity, capacity)
        for k in range(0, capacity, 2):
            pair = []
            for j in range(min(2, capacity - k)):
                place = second_ref[i * capacity + k + j]
                pair.append(jnp.concatenate([rows[r, place] for r in range(replicas)], axis=1))
            product = dot(jnp.concatenate(pair, axis=0), factors[1, places[i]])
            for j in range(len(pair)):
                result[i * capacity + k + j] = product[j * share : (j + 1) * share].astype(
                    jnp.bfloat16
                )
        copy = pltpu.make_async_copy(result.at[slots], out_ref.at[slots], out_sem.at[i])
        copy.start()
        out_copies.append(copy)
    for copy in out_copies:
        copy.wait()
    for copy in pending:
        copy.wait_send()


def permute_kernel(place_ref, in_ref, out_ref, buffer, in_sems, out_sems):
    blocks = in_ref.shape[0]
    loads = []
    for b in range(blocks):
        loads.append(
            pltpu.make_async_copy(in_ref.at[place_ref[b]], buffer.at[b], in_sems.at[b])
        )
        loads[b].start()
    stores = []
    for b in range(blocks):
        loads[b].wait()
        stores.append(pltpu.make_async_copy(buffer.at[b], out_ref.at[b], out_sems.at[b]))
        stores[b].start()
    for copy in stores:
        copy.wait()


def gather_factors(
    gradients,
    output_stats,
    input_stats,
    output_factor,
    output_inverse,
    input_factor,
    input_inverse,
    block_output,
    block_input,
    output_owner,
    input_owner,
):
    workers, replicas = lax.axis_size("work"), lax.axis_size("rep")
    blocks, order, cols = gradients.shape
    capacity = blocks // workers
    share = order // replicas
    work = lax.axis_index("work")
    at = jnp.arange(blocks, dtype=jnp.int32)

    def slots_of(labels, owner):
        labels = lax.dynamic_slice_in_dim(labels, work * blocks, blocks)
        dest = lookup(labels, owner ^ work)
        return dest * capacity + group_rank(dest)

    def by_slot(slot, values):
        return jnp.sum(jnp.where(slot[None, :] == at[:, None], values[None, :], 0), axis=1)

    out_slot = slots_of(block_output, output_owner)
    in_slot = slots_of(block_input, input_owner)
    first, second = by_slot(out_slot, at), by_slot(in_slot, out_slot)
    smem = pl.BlockSpec(memory_space=pltpu.SMEM)
    vmem = pl.BlockSpec(memory_space=pltpu.VMEM)
    hbm = pl.BlockSpec(memory_space=pl.ANY)
    sem = pltpu.SemaphoreType.DMA
    lines = workers // 2
    bf16 = jnp.bfloat16
    result = pl.pallas_call(
        functools.partial(fused_kernel, workers, replicas),
        out_shape=jax.ShapeDtypeStruct((blocks, share, order), bf16),
        in_specs=[smem] * 2 + [hbm] + [vmem] * 2 + [hbm] * 4,
        out_specs=hbm,
        scratch_shapes=[
            pltpu.VMEM(gradients.shape, bf16),
            pltpu.VMEM(output_factor.shape, jnp.float32),
            pltpu.VMEM(output_inverse.shape, jnp.float32),
            pltpu.VMEM(input_factor.shape, jnp.float32),
            pltpu.VMEM(input_inverse.shape, jnp.float32),
            pltpu.VMEM((2, replicas) + output_stats.shape[1:], bf16),
            pltpu.VMEM((2, workers, order, order), bf16),
            pltpu.VMEM((blocks, order, cols), bf16),
            pltpu.VMEM((replicas, blocks, share, cols), bf16),
            pltpu.VMEM((blocks, share, order), bf16),
            sem((2, replicas - 1)),
            sem((2, replicas - 1)),
            sem((2, lines - 1)),
            sem((2, lines - 1)),
            sem((2, lines)),
            sem((2, lines)),
            sem((2, workers)),
            sem((2, workers)),
            sem((workers, replicas - 1)),
            sem((workers, replicas - 1)),
            sem((workers,)),
            sem((5,)),
        ],
        compiler_params=pltpu.CompilerParams(
            collective_id=0, has_side_effects=True, vmem_limit_bytes=58 * 1024 * 1024
        ),
    )(
        first,
        second,
        gradients,
        output_stats,
        input_stats,
        output_factor,
        output_inverse,
        input_factor,
        input_inverse,
    )
    return pl.pallas_call(
        permute_kernel,
        out_shape=jax.ShapeDtypeStruct((blocks, share, order), bf16),
        in_specs=[smem, hbm],
        out_specs=hbm,
        scratch_shapes=[
            pltpu.VMEM((blocks, share, order), bf16),
            sem((blocks,)),
            sem((blocks,)),
        ],
        compiler_params=pltpu.CompilerParams(vmem_limit_bytes=56 * 1024 * 1024),
    )(in_slot, result)


def solution(mesh):
    in_specs = (
        P("work", None, "rep"),
        P("work", "rep", None),
        P("work", "rep", None),
        P("work", None, None),
        P("work", None, None),
        P("work", None, None),
        P("work", None, None),
        P(),
        P(),
        P(),
        P(),
    )
    out_specs = P("work", "rep", None)
    workers, replicas = mesh.shape["work"], mesh.shape["rep"]
    small = 4 <= workers <= 8 and replicas in (2, 4)
    local = gather_factors if small else exchange_blocks
    return jax.shard_map(local, mesh=mesh, in_specs=in_specs, out_specs=out_specs, check_vma=False)
```

```python
import functools

import jax
import jax.numpy as jnp
from jax import lax
from jax.experimental import pallas as pl
from jax.experimental.pallas import tpu as pltpu
from jax.sharding import PartitionSpec as P

decay_rate = 0.5


def refine(factor, inverse, samples):
    moment = jnp.dot(samples.T, samples, preferred_element_type=jnp.float32)
    updated = decay_rate * factor + (1.0 - decay_rate) / samples.shape[0] * moment
    product = jnp.dot(updated, inverse, precision=lax.Precision.HIGHEST)
    refined = 2.0 * inverse - jnp.dot(inverse, product, precision=lax.Precision.HIGHEST)
    return refined.astype(jnp.bfloat16)


def lookup(labels, values):
    matches = labels[:, None] == jnp.arange(values.shape[0], dtype=jnp.int32)[None, :]
    return jnp.sum(jnp.where(matches, values[None, :], 0), axis=1)


def group_rank(grouping):
    count = grouping.shape[0]
    positions = jnp.arange(count, dtype=jnp.int32)
    same_group = grouping[:, None] == grouping[None, :]
    earlier = positions[None, :] < positions[:, None]
    return jnp.sum(jnp.logical_and(same_group, earlier), axis=1)


def place_rows(target, data, out_count):
    selector = (jnp.arange(out_count, dtype=jnp.int32)[:, None] == target[None, :]).astype(
        jnp.bfloat16
    )
    return jnp.einsum("st,tij->sij", selector, data, preferred_element_type=jnp.float32).astype(
        jnp.bfloat16
    )


def pick_rows(source, data):
    selector = (source[:, None] == jnp.arange(data.shape[0], dtype=jnp.int32)[None, :]).astype(
        jnp.bfloat16
    )
    return jnp.einsum("st,tij->sij", selector, data, preferred_element_type=jnp.float32).astype(
        jnp.bfloat16
    )


def redirect(slot_count, holding, source_slot, target_slot):
    chosen = jnp.where(holding, source_slot, slot_count)
    return jnp.full((slot_count,), slot_count, jnp.int32).at[chosen].set(target_slot, mode="drop")


def relocate(buffer, target, slot_count):
    flat_view = buffer.reshape((slot_count,) + buffer.shape[2:])
    placed = place_rows(target, flat_view, slot_count)
    return placed.reshape(buffer.shape)


def exchange_blocks(
    gradients,
    output_stats,
    input_stats,
    output_factor,
    output_inverse,
    input_factor,
    input_inverse,
    block_output,
    block_input,
    output_owner,
    input_owner,
):
    workers = lax.axis_size("work")
    local_blocks, block_order, shard_cols = gradients.shape
    total_blocks = block_output.shape[0]
    capacity = (local_blocks + workers - 1) // workers
    slot_count = workers * capacity
    worker_index = lax.axis_index("work")
    home_index = jnp.arange(total_blocks, dtype=jnp.int32) // local_blocks
    out_dest = lookup(block_output, output_owner)
    in_dest = lookup(block_input, input_owner)
    first_rank = group_rank(home_index * workers + out_dest)
    second_rank = group_rank(out_dest * workers + in_dest)
    third_rank = group_rank(in_dest * workers + home_index)
    gathered_out, gathered_in = (
        lax.all_gather(output_stats, "rep", axis=1, tiled=True),
        lax.all_gather(input_stats, "rep", axis=1, tiled=True),
    )
    left_inverse = refine(output_factor[0], output_inverse[0], gathered_out[0])
    right_inverse = refine(input_factor[0], input_inverse[0], gathered_in[0])
    own_places = lax.dynamic_slice_in_dim(
        out_dest * capacity + first_rank, worker_index * local_blocks, local_blocks
    )
    outgoing = place_rows(own_places, gradients, slot_count)
    outgoing = outgoing.reshape(workers, capacity, block_order, shard_cols)
    arrived = jnp.einsum(
        "ij,nkjc->nkic",
        left_inverse,
        lax.all_to_all(outgoing, "work", split_axis=0, concat_axis=0, tiled=True),
        preferred_element_type=jnp.float32,
    ).astype(jnp.bfloat16)
    second_target = redirect(
        slot_count,
        out_dest == worker_index,
        home_index * capacity + first_rank,
        in_dest * capacity + second_rank,
    )
    forward = relocate(arrived, second_target, slot_count)
    third_target = redirect(
        slot_count,
        in_dest == worker_index,
        out_dest * capacity + second_rank,
        home_index * capacity + third_rank,
    )
    rows_form = lax.all_to_all(forward, "rep", split_axis=2, concat_axis=3, tiled=True)
    finished = jnp.einsum(
        "nkrc,cd->nkrd",
        lax.all_to_all(rows_form, "work", split_axis=0, concat_axis=0, tiled=True),
        right_inverse,
        preferred_element_type=jnp.float32,
    ).astype(jnp.bfloat16)
    backward = relocate(finished, third_target, slot_count)
    returned = lax.all_to_all(backward, "work", split_axis=0, concat_axis=0, tiled=True)
    returned = returned.reshape((slot_count,) + returned.shape[2:])
    own_slots = lax.dynamic_slice_in_dim(
        in_dest * capacity + third_rank, worker_index * local_blocks, local_blocks
    )
    return pick_rows(own_slots, returned)


def flip(value, mask):
    result, bit = value, 1
    while bit <= mask:
        if mask & bit:
            result = result + bit - 2 * bit * ((value // bit) % 2)
        bit *= 2
    return result


def halves(x):
    high = x.astype(jnp.bfloat16)
    return high, (x - high.astype(jnp.float32)).astype(jnp.bfloat16)


def dot(a, b):
    return jnp.dot(a, b, preferred_element_type=jnp.float32)


def exact_dot(a, b):
    return dot(a[0], b[0]) + (dot(a[0], b[1]) + dot(a[1], b[0]))


def fused_kernel(
    workers,
    replicas,
    first_ref,
    second_ref,
    g_hbm,
    os_ref,
    is_ref,
    of_hbm,
    oi_hbm,
    if_hbm,
    ii_hbm,
    out_ref,
    g_ref,
    of_ref,
    oi_ref,
    if_ref,
    ii_ref,
    stats,
    factors,
    middle,
    rows,
    result,
    stat_send,
    stat_recv,
    z_send,
    z_recv,
    y_send,
    y_recv,
    s_send,
    s_recv,
    m_send,
    m_recv,
    out_sem,
    load_sem,
):
    work, rep = lax.axis_index("work"), lax.axis_index("rep")
    blocks, order, cols = g_ref.shape
    capacity = blocks // workers
    lines = workers // 2
    share = order // replicas
    half = order // 2
    core = rep % 2
    sibling = {"rep": flip(rep, 1)}
    pending = []

    sources = (of_hbm, oi_hbm, if_hbm, ii_hbm, g_hbm)
    targets = (of_ref, oi_ref, if_ref, ii_ref, g_ref)
    loads = []
    for n, (source, target) in enumerate(zip(sources, targets)):
        loads.append(pltpu.make_async_copy(source, target, load_sem.at[n]))
        loads[n].start()

    barrier = pltpu.get_barrier_semaphore()
    peers = [{"rep": flip(rep, d)} for d in range(1, replicas)]
    peers += [{"work": flip(work, 1)}] + [{"work": flip(work, 2 * d)} for d in range(1, lines)]
    for peer in peers:
        pl.semaphore_signal(barrier, inc=1, device_id=peer, device_id_type=pl.DeviceIdType.MESH)
    pl.semaphore_wait(barrier, len(peers))

    def push(src, dst, send, recv, peer):
        copy = pltpu.make_async_remote_copy(
            src_ref=src,
            dst_ref=dst,
            send_sem=send,
            recv_sem=recv,
            device_id=peer,
            device_id_type=pl.DeviceIdType.MESH,
        )
        copy.start()
        pending.append(copy)
        return copy

    stat_copies = []
    for t, ref in enumerate((os_ref, is_ref)):
        for d in range(1, replicas):
            stat_copies.append(
                push(
                    ref.at[0],
                    stats.at[t, rep],
                    stat_send.at[t, d - 1],
                    stat_recv.at[t, d - 1],
                    {"rep": flip(rep, d)},
                )
            )
        stats[t, rep] = ref[0]

    mine = pl.ds(pl.multiple_of(core * half, half), half)
    places = [flip(work, i) for i in range(workers)]

    def chunk(t, i):
        return factors.at[t, places[i], mine]

    def refine_half(t, f_ref, i_ref):
        for copy in stat_copies[t * (replicas - 1) : (t + 1) * (replicas - 1)]:
            copy.wait_recv()
        loads[2 * t].wait()
        loads[2 * t + 1].wait()
        sample = stats[t].reshape(-1, order)
        moment = lax.dot_general(
            sample, sample, (((0,), (0,)), ((), ())), preferred_element_type=jnp.float32
        )
        updated = decay_rate * f_ref[0] + (1.0 - decay_rate) / sample.shape[0] * moment
        own = i_ref[0, mine]
        product = exact_dot(halves(own), halves(updated))
        refined = 2.0 * own - exact_dot(halves(product), halves(i_ref[0]))
        factors[t, places[0], mine] = refined.astype(jnp.bfloat16)

    z_copies, y_copies, s_copies = {}, {}, {}

    def to_sibling(t, i):
        s_copies[t, i] = push(chunk(t, i), chunk(t, i), s_send.at[t, i], s_recv.at[t, i], sibling)

    def to_y(t, d):
        y_copies[t, d] = push(
            chunk(t, 2 * d),
            chunk(t, 2 * d),
            y_send.at[t, d],
            y_recv.at[t, d],
            {"work": places[1]},
        )

    def to_z(t):
        for d in range(1, lines):
            z_copies[t, d] = push(
                chunk(t, 0),
                chunk(t, 0),
                z_send.at[t, d - 1],
                z_recv.at[t, d - 1],
                {"work": places[2 * d]},
            )

    m_copies = []
    own_rows = pl.ds(pl.multiple_of(rep * share, share), share)

    def left_multiply(i):
        slots = pl.ds(i * capacity, capacity)
        wide = jnp.concatenate(
            [g_ref[first_ref[i * capacity + k]] for k in range(capacity)], axis=1
        )
        for j in range(2):
            part = pl.ds(j * half, half)
            product = dot(factors[0, places[i], part], wide).astype(jnp.bfloat16)
            for k in range(capacity):
                middle[i * capacity + k, part] = product[:, k * cols : (k + 1) * cols]
        for d in range(replicas - 1, 0, -1):
            other = flip(rep, d)
            m_copies.append(
                push(
                    middle.at[slots, pl.ds(pl.multiple_of(other * share, share), share)],
                    rows.at[rep, slots],
                    m_send.at[i, d - 1],
                    m_recv.at[i, d - 1],
                    {"rep": other},
                )
            )
        rows[rep, slots] = middle[slots, own_rows]

    def spread(t, ready):
        queue = []
        for d in range(1, lines + 1):
            if d < lines:
                z_copies[t, d].wait_recv()
                to_y(t, d)
                to_sibling(t, 2 * d)
                if d == lines - 1 and t == 0:
                    to_y(1, 0)
                    to_z(1)
                    to_sibling(1, 0)
            while queue:
                i = queue.pop(0)
                s_copies[t, i].wait_recv()
                ready(i)
            y_copies[t, d - 1].wait_recv()
            to_sibling(t, 2 * d - 1)
            if d < lines:
                queue.append(2 * d)
            queue.append(2 * d - 1)
        for i in queue:
            s_copies[t, i].wait_recv()
            ready(i)

    refine_half(0, of_ref, oi_ref)
    to_y(0, 0)
    to_z(0)
    to_sibling(0, 0)
    loads[4].wait()
    s_copies[0, 0].wait_recv()
    left_multiply(0)
    refine_half(1, if_ref, ii_ref)
    spread(0, left_multiply)
    s_copies[1, 0].wait_recv()
    spread(1, lambda i: None)
    for copy in m_copies:
        copy.wait_recv()
    out_copies = []
    for i in range(workers):
        slots = pl.ds(i * capacity, capacity)
        for k in range(0, capacity, 2):
            pair = []
            for j in range(min(2, capacity - k)):
                place = second_ref[i * capacity + k + j]
                pair.append(jnp.concatenate([rows[r, place] for r in range(replicas)], axis=1))
            product = dot(jnp.concatenate(pair, axis=0), factors[1, places[i]])
            for j in range(len(pair)):
                result[i * capacity + k + j] = product[j * share : (j + 1) * share].astype(
                    jnp.bfloat16
                )
        copy = pltpu.make_async_copy(result.at[slots], out_ref.at[slots], out_sem.at[i])
        copy.start()
        out_copies.append(copy)
    for copy in out_copies:
        copy.wait()
    for copy in pending:
        copy.wait_send()


def permute_kernel(place_ref, in_ref, out_ref, buffer, in_sems, out_sems):
    blocks = in_ref.shape[0]
    loads = []
    for b in range(blocks):
        loads.append(
            pltpu.make_async_copy(in_ref.at[place_ref[b]], buffer.at[b], in_sems.at[b])
        )
        loads[b].start()
    stores = []
    for b in range(blocks):
        loads[b].wait()
        stores.append(pltpu.make_async_copy(buffer.at[b], out_ref.at[b], out_sems.at[b]))
        stores[b].start()
    for copy in stores:
        copy.wait()


def gather_factors(
    gradients,
    output_stats,
    input_stats,
    output_factor,
    output_inverse,
    input_factor,
    input_inverse,
    block_output,
    block_input,
    output_owner,
    input_owner,
):
    workers, replicas = lax.axis_size("work"), lax.axis_size("rep")
    blocks, order, cols = gradients.shape
    capacity = blocks // workers
    share = order // replicas
    work = lax.axis_index("work")
    at = jnp.arange(blocks, dtype=jnp.int32)

    def slots_of(labels, owner):
        homes = jnp.arange(workers, dtype=jnp.int32)[:, None]
        labels = jnp.sum(jnp.where(homes == work, labels.reshape(workers, blocks), 0), axis=0)
        dest = lookup(labels, owner ^ work)
        return dest * capacity + group_rank(dest)

    def by_slot(slot, values):
        return jnp.sum(jnp.where(slot[None, :] == at[:, None], values[None, :], 0), axis=1)

    out_slot = slots_of(block_output, output_owner)
    in_slot = slots_of(block_input, input_owner)
    first, second = by_slot(out_slot, at), by_slot(in_slot, out_slot)
    smem = pl.BlockSpec(memory_space=pltpu.SMEM)
    vmem = pl.BlockSpec(memory_space=pltpu.VMEM)
    hbm = pl.BlockSpec(memory_space=pl.ANY)
    sem = pltpu.SemaphoreType.DMA
    lines = workers // 2
    bf16 = jnp.bfloat16
    result = pl.pallas_call(
        functools.partial(fused_kernel, workers, replicas),
        out_shape=jax.ShapeDtypeStruct((blocks, share, order), bf16),
        in_specs=[smem] * 2 + [hbm] + [vmem] * 2 + [hbm] * 4,
        out_specs=hbm,
        scratch_shapes=[
            pltpu.VMEM(gradients.shape, bf16),
            pltpu.VMEM(output_factor.shape, jnp.float32),
            pltpu.VMEM(output_inverse.shape, jnp.float32),
            pltpu.VMEM(input_factor.shape, jnp.float32),
            pltpu.VMEM(input_inverse.shape, jnp.float32),
            pltpu.VMEM((2, replicas) + output_stats.shape[1:], bf16),
            pltpu.VMEM((2, workers, order, order), bf16),
            pltpu.VMEM((blocks, order, cols), bf16),
            pltpu.VMEM((replicas, blocks, share, cols), bf16),
            pltpu.VMEM((blocks, share, order), bf16),
            sem((2, replicas - 1)),
            sem((2, replicas - 1)),
            sem((2, lines - 1)),
            sem((2, lines - 1)),
            sem((2, lines)),
            sem((2, lines)),
            sem((2, workers)),
            sem((2, workers)),
            sem((workers, replicas - 1)),
            sem((workers, replicas - 1)),
            sem((workers,)),
            sem((5,)),
        ],
        compiler_params=pltpu.CompilerParams(
            collective_id=0, has_side_effects=True, vmem_limit_bytes=58 * 1024 * 1024
        ),
    )(
        first,
        second,
        gradients,
        output_stats,
        input_stats,
        output_factor,
        output_inverse,
        input_factor,
        input_inverse,
    )
    return pl.pallas_call(
        permute_kernel,
        out_shape=jax.ShapeDtypeStruct((blocks, share, order), bf16),
        in_specs=[smem, hbm],
        out_specs=hbm,
        scratch_shapes=[
            pltpu.VMEM((blocks, share, order), bf16),
            sem((blocks,)),
            sem((blocks,)),
        ],
        compiler_params=pltpu.CompilerParams(vmem_limit_bytes=56 * 1024 * 1024),
    )(in_slot, result)


def solution(mesh):
    in_specs = (
        P("work", None, "rep"),
        P("work", "rep", None),
        P("work", "rep", None),
        P("work", None, None),
        P("work", None, None),
        P("work", None, None),
        P("work", None, None),
        P(),
        P(),
        P(),
        P(),
    )
    out_specs = P("work", "rep", None)
    workers, replicas = mesh.shape["work"], mesh.shape["rep"]
    small = 4 <= workers <= 8 and replicas in (2, 4)
    local = gather_factors if small else exchange_blocks
    return jax.shard_map(local, mesh=mesh, in_specs=in_specs, out_specs=out_specs, check_vma=False)
```
